512 devices in a mesh: row: 32 (over y, x, core), col: 16 (over z).
Axes of the slice: x: 4, y: 4, z: 16, core: 2. Of those that a mesh axis runs over, the one named last changes fastest.
Arguments:
- iterate_t: bfloat16 [32, 16, 64, 32768], P(None, 'col', None, 'row'), may hold values from -0.03125 to 0.03125
- vectors: bfloat16 [32768, 256], P(('row', 'col')), may hold values from -6 to 6
- old_factor_t: bfloat16 [512, 32768], P('col', 'row'), may hold values from -5 to 5
Outputs:
- panel: float32 [32768, 256], P(('row', 'col'))
- basis: float32 [768, 32768], P('col', 'row')
The draws below stay inside these ranges and needn't reach their ends.
All inputs are finite; a program needn't handle non-finite values.
Results may differ from the reference program's by a relative error of at most 0.0013.
Values may be sent and summed in bfloat16 or wider, within the bound.
A program may use at most 64 MiB of HBM per device.

```python
import jax
import jax.numpy as jnp
from jax import lax

NSTATE = 32768
PANEL = 256
OLD = 512
FACTOR = 768
STRIPS = 32
GROUPS = 16
CB = 64


def draw_old_factor_t(key, part):
    noise_key, shared_key = jax.random.split(jax.random.fold_in(key, 7))
    noise = jax.random.truncated_normal(noise_key, -4.0, 4.0, (OLD, NSTATE), jnp.float32)
    shared = jax.random.normal(shared_key, (1, NSTATE), jnp.float32)
    values = jnp.clip(noise + 0.6 * shared, -5.0, 5.0)
    return values.astype(jnp.bfloat16)


def steps_of(own_key, dims, cuts, smallest, high):
    level, own = 1.0, jax.random.fold_in(own_key, 6)
    for axis_at, blocks in cuts:
        draws = jnp.exp(jax.random.uniform(jax.random.fold_in(own, axis_at), (blocks,), jnp.float32, smallest / len(cuts), high / len(cuts)))
        level = level * jnp.repeat(draws, dims[axis_at] // blocks).reshape([-1 if axis == axis_at else 1 for axis in range(len(dims))])
    return level


def gaussian(stream_key, extent, spread, bound, cuts=(), kind=jnp.bfloat16):
    loudness = steps_of(stream_key, extent, cuts, -0.22, 0.18) if cuts else 1.0
    entries = jax.random.normal(stream_key, extent, jnp.float32) * spread * loudness
    return jnp.minimum(jnp.maximum(entries, -bound), bound).astype(kind)


def setup_inputs(seed: int = 0) -> dict:
    streams_of = jax.random.split(jax.random.key(seed), 4)
    return {
        "iterate_t": gaussian(streams_of[0], (STRIPS, GROUPS, CB, NSTATE), NSTATE ** -0.5, 0.03125, ((1, 16), (3, 32))),
        "vectors": gaussian(streams_of[1], (NSTATE, PANEL), 1.0, 6.0, ((0, 512),)),
        "old_factor_t": draw_old_factor_t(jax.random.fold_in(streams_of[3], 71), 0),
    }


def reference(iterate_t, vectors, old_factor_t):
    flat_iterate = iterate_t.reshape(NSTATE, NSTATE)
    slab_width = min(1024, NSTATE)

    def apply_iterate(vector):
        vector_full = vector.astype(jnp.float32)

        def one_slab(first_row):
            column_slab = lax.dynamic_slice_in_dim(flat_iterate, first_row, slab_width, 1).astype(jnp.float32)
            return lax.dot_general(column_slab, vector_full, (((0,), (0,)), ((), ())), precision=lax.Precision.HIGHEST)
        slab_starts = (jnp.arange(NSTATE // slab_width) * slab_width).astype(jnp.int32)
        return lax.map(one_slab, slab_starts).reshape(NSTATE, PANEL)
    first_full = apply_iterate(vectors)
    second = apply_iterate(first_full.astype(jnp.bfloat16)).astype(jnp.bfloat16)
    panel = 1.5 * first_full - 0.5 * apply_iterate(second)
    old_full = old_factor_t.astype(jnp.float32)
    old_old = jnp.dot(old_full, old_full.T, precision=lax.Precision.HIGHEST)
    old_panel = jnp.dot(old_full, panel, precision=lax.Precision.HIGHEST)
    panel_panel = jnp.dot(panel.T, panel, precision=lax.Precision.HIGHEST)
    gram = jnp.concatenate([jnp.concatenate([old_old, old_panel], 1), jnp.concatenate([old_panel.T, panel_panel], 1)], 0) * (1.0 / NSTATE)
    lower_factor = jnp.linalg.cholesky(gram)
    identity = jnp.eye(FACTOR, dtype=jnp.float32)
    inverse = jax.scipy.linalg.solve_triangular(lower_factor, identity, lower=True)
    basis = jnp.dot(inverse[:, :OLD], old_full, precision=lax.Precision.HIGHEST)
    basis = basis + jnp.dot(inverse[:, OLD:], panel.T, precision=lax.Precision.HIGHEST)
    return (panel, basis)
```

```python
import functools

import jax
import jax.numpy as jnp
from jax import lax
from jax.experimental import pallas as pl
from jax.experimental.pallas import tpu as pltpu
from jax.sharding import PartitionSpec as P

NSTATE = 32768
MESH = pl.DeviceIdType.MESH
HIGHEST = lax.Precision.HIGHEST
BF = jnp.bfloat16
F32 = jnp.float32
NT = (((1,), (1,)), ((), ()))


def split3(a):
    hi = a.astype(BF)
    rest = a - hi.astype(F32)
    mid = rest.astype(BF)
    low = (rest - mid.astype(F32)).astype(BF)
    return hi, mid, low


def comm_kernel(
    x, v, old, panel_o, oldall, pall, aout, bcout,
    xt, vsend, vg, part, bufr, bufl, first,
    apart, asib, ash, apl, bcpart, bcsib, bcs, bcr, bcz, zsh, fsh,
    ag_s, ag_r, fw_s, fw_r, rs_s, rs_r, og_s, og_r, pg_s, pg_r, az_s, az_r,
    a_s, a_r, b_s, b_r,
):
    row = lax.axis_index("row")
    z = lax.axis_index("col")
    chip = row // 2
    core = row % 2
    sib = (chip * 2 + 1 - core, z)
    right = (row, (z + 1) % 16)
    left = (row, (z + 15) % 16)

    def plane(d):
        y = (chip // 4 + d // 4) % 4
        w = (chip % 4 + d % 4) % 4
        return y * 4 + w

    def remote(src, dst, ssem, rsem, target):
        return pltpu.make_async_remote_copy(
            src_ref=src, dst_ref=dst, send_sem=ssem, recv_sem=rsem, device_id=target, device_id_type=MESH
        )

    barrier = pltpu.get_barrier_semaphore()

    @pl.loop(1, 16)
    def _(d):
        pl.semaphore_signal(barrier, inc=1, device_id=(plane(d) * 2 + core, z), device_id_type=MESH)
        pl.semaphore_signal(barrier, inc=1, device_id=(row, (z + d) % 16), device_id_type=MESH)

    pl.semaphore_signal(barrier, inc=1, device_id=sib, device_id_type=MESH)

    @pl.loop(0, 16)
    def _(t):
        a = (t % 8) * 4 + t // 8
        pair = jnp.concatenate([x[a, 0], x[a + 2, 0]], 0)
        xt[:, pl.ds(pl.multiple_of(t * 128, 128), 128)] = pair.T

    pl.semaphore_wait(barrier, 31)

    def plane_push(src, dst, ssem, rsem):
        @pl.loop(1, 16)
        def _(d):
            remote(src, dst, ssem, rsem, (plane(d) * 2 + core, z)).start()

    def bulk(ref, ssem, rsem):
        return remote(ref.at[pl.ds(0, 15)], ref.at[pl.ds(0, 15)], ssem, rsem, sib)

    def gather_start(m):
        plane_push(vsend.at[m], vg.at[m, core * 16 + chip], ag_s.at[m], ag_r.at[m])
        vg[m, core * 16 + chip] = vsend[m]

    def product(m, half, add):
        rhs = vg[m, pl.ds(half * 16, 16)].reshape(1024, 256)
        for rb in range(2):
            lhs = xt[pl.ds(rb * 512, 512), pl.ds(pl.multiple_of(half * 1024, 1024), 1024)]
            res = jnp.dot(lhs, rhs, preferred_element_type=F32).reshape(8, 64, 256)
            if add:
                part[m, pl.ds(rb * 8, 8)] += res
            else:
                part[m, pl.ds(rb * 8, 8)] = res

    def gather_product(m):
        wait = bulk(vg.at[m], ag_s.at[m], ag_r.at[m])
        wait.wait_recv()
        span = vg.at[m, pl.ds(core * 16, 16)]
        forward = remote(span, span, fw_s.at[m], fw_r.at[m], sib)
        forward.start()
        product(m, core, False)
        forward.wait_recv()
        product(m, 1 - core, True)
        wait.wait_send()
        forward.wait_send()

    def rs_copy(m, way, s):
        buf, to = (bufr, right) if way == 0 else (bufl, left)
        dest = (z + 8 - s) % 16 if way == 0 else (z + 9 + s) % 16
        return remote(part.at[m, dest], buf.at[m, s], rs_s.at[m, way, s], rs_r.at[m, way, s], to), dest

    def reduce_scatter(m, hook):
        for way in (0, 1):
            rs_copy(m, way, 0)[0].start()
        for s in range(1, 8):
            for way in (0, 1):
                if way == 1 and s == 7:
                    continue
                rs_copy(m, way, s - 1)[0].wait_recv()
                copy, dest = rs_copy(m, way, s)
                buf = bufr if way == 0 else bufl
                part[m, dest] += buf[m, s - 1]
                copy.start()
            hook(s)
        rs_copy(m, 1, 6)[0].wait_recv()
        rs_copy(m, 0, 7)[0].wait_recv()
        res = part[m, z] + bufr[m, 7] + bufl[m, 6]
        for s in range(8):
            rs_copy(m, 0, s)[0].wait_send()
            if s < 7:
                rs_copy(m, 1, s)[0].wait_send()
        return res

    def ring(own, blocks, ssem, rsem):
        def copy(way, s):
            idx = (z - s + 16) % 16 if way == 0 else (z + s) % 16
            return remote(
                own if s == 0 else blocks.at[idx], blocks.at[idx], ssem.at[way, s], rsem.at[way, s],
                right if way == 0 else left,
            )

        def step(s):
            for way in (0, 1):
                if s > 0 and not (way == 1 and s == 8):
                    copy(way, s - 1).wait_recv()
                if s < 8 and not (way == 1 and s == 7):
                    copy(way, s).start()

        def finish():
            for s in range(8):
                copy(0, s).wait_send()
                if s < 7:
                    copy(1, s).wait_send()

        return step, finish

    vsend[0] = v[...]
    gather_start(0)
    old_step, old_finish = ring(old, oldall, og_s, og_r)
    old_step(0)
    oldall[z] = old[...]
    gather_product(0)

    def hook0(s):
        old_step(s)

    first_full = reduce_scatter(0, hook0)
    first[...] = first_full
    vsend[1] = first_full.astype(BF)
    gather_start(1)
    old_step(8)
    old_finish()

    every = oldall[...].reshape(512, 1024)
    share = lax.dot_general(old[...], every, NT, preferred_element_type=F32)
    apart[...] = share.reshape(2, 16, 512)
    a_sib = remote(apart.at[1 - core], asib, a_s.at[0], a_r.at[0], sib)
    a_sib.start()
    gather_product(1)
    a_sib.wait_recv()
    ash[...] = apart[core] + asib[...]
    plane_push(ash, apl.at[chip], a_s.at[1], a_r.at[1])
    apl[chip] = ash[...]
    a_wait = bulk(apl, a_s.at[1], a_r.at[1])
    a_step, a_finish = ring(aout.at[core, z], aout.at[core], az_s, az_r)

    def hook1(s):
        if s == 3:
            a_wait.wait_recv()
            total = apl[0]
            for q in range(1, 16):
                total = total + apl[q]
            aout[core, z] = total * (1.0 / NSTATE)
        if s >= 3:
            a_step(s - 3)

    second = reduce_scatter(1, hook1)
    vsend[2] = second.astype(BF)
    gather_start(2)
    a_step(5)
    gather_product(2)

    a_half = aout.at[core]
    a_forward = remote(a_half, a_half, a_s.at[2], a_r.at[2], sib)

    def hook2(s):
        if s <= 3:
            a_step(5 + s)
        if s == 4:
            a_forward.start()

    third = reduce_scatter(2, hook2)
    panel = 1.5 * first[...] - 0.5 * third
    panel_o[...] = panel
    p_step, p_finish = ring(panel_o, pall, pg_s, pg_r)
    p_step(0)
    pall[z] = panel

    side = z % 2
    doubled = jnp.concatenate([panel, panel], 0)
    rows = lax.broadcasted_iota(jnp.int32, (128, 256), 0)
    doubled = jnp.where(rows // 64 == side, doubled, 0.0).T
    window = oldall[:, :, pl.ds(pl.multiple_of((z // 2) * 128, 128), 128)].reshape(512, 128)
    cross = sum(lax.dot_general(t, window, NT, preferred_element_type=F32) for t in split3(doubled))
    square = lax.dot_general(doubled, doubled, NT, precision=HIGHEST, preferred_element_type=F32)
    bcpart[:, :, :, pl.ds(0, 512)] = cross.reshape(2, 16, 8, 512)
    bcpart[:, :, :, pl.ds(512, 256)] = square.reshape(2, 16, 8, 256)
    b_sib = remote(bcpart.at[1 - core], bcsib, b_s.at[0], b_r.at[0], sib)
    b_sib.start()
    p_step(1)
    b_sib.wait_recv()
    bcs[...] = bcpart[core] + bcsib[...]

    @pl.loop(1, 16)
    def _(d):
        q = plane(d)
        remote(bcs.at[q], bcr.at[chip], b_s.at[1], b_r.at[1], (q * 2 + core, z)).start()

    bcr[chip] = bcs[chip]
    p_step(2)
    p_step(3)
    b_rs = bulk(bcr, b_s.at[1], b_r.at[1])
    b_rs.wait_recv()
    total = bcr[0]
    for q in range(1, 16):
        total = total + bcr[q]
    zsh[...] = total

    @pl.loop(1, 16)
    def _(d):
        remote(zsh, bcz.at[z], b_s.at[2], b_r.at[2], (row, (z + d) % 16)).start()

    bcz[z] = zsh[...]
    p_step(4)
    p_step(5)
    p_step(6)
    b_z = bulk(bcz, b_s.at[2], b_r.at[2])
    b_z.wait_recv()
    total = bcz[0]
    for q in range(1, 16):
        total = total + bcz[q]
    fsh[...] = total * (1.0 / NSTATE)
    plane_push(fsh, bcout.at[core, chip], b_s.at[3], b_r.at[3])
    bcout[core, chip] = fsh[...]
    p_step(7)
    b_ag = bulk(bcout.at[core], b_s.at[3], b_r.at[3])
    b_ag.wait_recv()
    b_half = bcout.at[core]
    b_forward = remote(b_half, b_half, b_s.at[4], b_r.at[4], sib)
    b_forward.start()
    p_step(8)
    p_finish()
    a_finish()
    a_sib.wait_send()
    a_wait.wait_send()
    a_forward.wait_recv()
    a_forward.wait_send()
    b_sib.wait_send()
    b_rs.wait_send()
    b_z.wait_send()
    b_ag.wait_send()
    b_forward.wait_recv()
    b_forward.wait_send()


def inverse_factor(block):
    n = 128
    rows = lax.broadcasted_iota(jnp.int32, (n, n), 0)
    lanes = lax.broadcasted_iota(jnp.int32, (n, n), 1)

    def eight(g, m):
        live = rows < n - 8 * g
        for s in range(8):
            column = m[:, s : s + 1]
            pivot_row = m[s : s + 1, :]
            pivot = m[s : s + 1, s : s + 1]
            factor = jnp.where(live & (rows > s), jnp.broadcast_to(column / pivot, (n, n)), 0.0)
            here = lanes == s
            line = jnp.where(here[s : s + 1, :], 1.0, pivot_row)
            m = jnp.where(here & live & (rows > s), 0.0, m) - factor * line
        m = jnp.concatenate([m[8:], m[:8]], 0)
        return pltpu.roll(m, n - 8, 1)

    m = lax.fori_loop(0, n // 8, eight, block)
    pivots = jnp.sum(jnp.where(rows == lanes, m, 0.0), axis=1, keepdims=True)
    unit = jnp.where(lanes < rows, m, jnp.where(lanes == rows, 1.0, 0.0))
    return unit * lax.rsqrt(pivots)


def basis_kernel(aout, bcout, oldall, pall, basis_o, gram, inv):
    z = lax.axis_index("col")

    @pl.loop(0, 16)
    def _(c):
        for h in range(2):
            gram[pl.ds(pl.multiple_of(c * 32 + h * 16, 16), 16), pl.ds(0, 512)] = aout[h, c]

    gram[pl.ds(512, 256), :] = bcout[...].reshape(256, 768)
    inv[...] = jnp.zeros((768, 768), F32)

    def dot(a, b):
        return jnp.dot(a, b, precision=HIGHEST, preferred_element_type=F32)

    def dot_nt(a, b):
        return lax.dot_general(a, b, NT, precision=HIGHEST, preferred_element_type=F32)

    for j in range(6):
        lo, hi = j * 128, (j + 1) * 128
        w = inverse_factor(gram[lo:hi, lo:hi])
        inv[lo:hi, lo:hi] = w
        if j > 0:
            inv[lo:hi, 0:lo] = dot(w, inv[lo:hi, 0:lo])
        if j < 5:
            factor = dot_nt(gram[hi:, lo:hi], w)
            for k in range(j + 1, 6):
                top = (k - j - 1) * 128
                gram[k * 128 :, k * 128 : (k + 1) * 128] -= dot_nt(factor[top:], factor[top : top + 128])
            inv[hi:, 0:hi] -= dot(factor, inv[lo:hi, 0:hi])

    mine = inv[pl.ds(pl.multiple_of(z * 48, 16), 48), :]
    every = oldall[...].reshape(512, 1024)
    res = dot_nt(mine[:, 512:], pall[...].reshape(1024, 256))
    for t in split3(mine[:, :512]):
        res = res + jnp.dot(t, every, preferred_element_type=F32)
    basis_o[...] = res


def body(iterate_t, vectors, old_factor_t):
    vm = pl.BlockSpec(memory_space=pltpu.VMEM)
    dma = pltpu.SemaphoreType.DMA
    out = jax.ShapeDtypeStruct
    panel, oldall, pall, aout, bcout = pl.pallas_call(
        comm_kernel,
        out_shape=(
            out((64, 256), F32),
            out((16, 32, 1024), BF),
            out((16, 64, 256), F32),
            out((2, 16, 16, 512), F32),
            out((2, 16, 8, 768), F32),
        ),
        in_specs=[vm] * 3,
        out_specs=(vm,) * 5,
        scratch_shapes=[
            pltpu.VMEM((1024, 2048), BF),
            pltpu.VMEM((3, 64, 256), BF),
            pltpu.VMEM((3, 32, 64, 256), BF),
            pltpu.VMEM((3, 16, 64, 256), F32),
            pltpu.VMEM((3, 8, 64, 256), F32),
            pltpu.VMEM((3, 7, 64, 256), F32),
            pltpu.VMEM((64, 256), F32),
            pltpu.VMEM((2, 16, 512), F32),
            pltpu.VMEM((16, 512), F32),
            pltpu.VMEM((16, 512), F32),
            pltpu.VMEM((16, 16, 512), F32),
            pltpu.VMEM((2, 16, 8, 768), F32),
            pltpu.VMEM((16, 8, 768), F32),
            pltpu.VMEM((16, 8, 768), F32),
            pltpu.VMEM((16, 8, 768), F32),
            pltpu.VMEM((16, 8, 768), F32),
            pltpu.VMEM((8, 768), F32),
            pltpu.VMEM((8, 768), F32),
            dma((3,)), dma((3,)), dma((3,)), dma((3,)),
            dma((3, 2, 8)), dma((3, 2, 8)),
            dma((2, 8)), dma((2, 8)),
            dma((2, 8)), dma((2, 8)),
            dma((2, 8)), dma((2, 8)),
            dma((3,)), dma((3,)),
            dma((5,)), dma((5,)),
        ],
        compiler_params=pltpu.CompilerParams(
            collective_id=0, has_side_effects=True, vmem_limit_bytes=48 << 20
        ),
        name="sign_step",
    )(iterate_t, vectors, old_factor_t)
    basis = pl.pallas_call(
        basis_kernel,
        out_shape=out((48, 1024), F32),
        in_specs=[vm] * 4,
        out_specs=vm,
        scratch_shapes=[pltpu.VMEM((768, 768), F32), pltpu.VMEM((768, 768), F32)],
        compiler_params=pltpu.CompilerParams(vmem_limit_bytes=48 << 20),
        name="recompress",
    )(aout, bcout, oldall, pall)
    return panel, basis


def solution(mesh):
    return jax.shard_map(
        body,
        mesh=mesh,
        in_specs=(P(None, "col", None, "row"), P(("row", "col"), None), P("col", "row")),
        out_specs=(P(("row", "col"), None), P("col", "row")),
        check_vma=False,
    )
```

```python
import functools

import jax
import jax.numpy as jnp
from jax import lax
from jax.experimental import pallas as pl
from jax.experimental.pallas import tpu as pltpu
from jax.sharding import PartitionSpec as P

NSTATE = 32768
MESH = pl.DeviceIdType.MESH
HIGHEST = lax.Precision.HIGHEST
BF = jnp.bfloat16
F32 = jnp.float32
NT = (((1,), (1,)), ((), ()))


def split3(a):
    hi = a.astype(BF)
    rest = a - hi.astype(F32)
    mid = rest.astype(BF)
    low = (rest - mid.astype(F32)).astype(BF)
    return hi, mid, low


def eight(g, m, out):
    n = 128
    sub = lax.broadcasted_iota(jnp.int32, (8, n), 0)
    lane = lax.broadcasted_iota(jnp.int32, (8, n), 1)
    c = [jnp.broadcast_to(m[:8, 8 + k : 9 + k], (8, n)) for k in range(8)]
    turned = pltpu.roll(m, n - 8, 1)
    top = jnp.where(lane < 8, jnp.where(lane == sub, 1.0, 0.0), turned[:8])
    lines, steps, pivots = [], [], c[0]
    for s in range(8):
        if s:
            pivots = jnp.where(sub == s, c[s], pivots)
        inv = 1.0 / c[s][s : s + 1, :]
        line = top[s : s + 1, :] * inv
        col = jnp.where(sub > s, c[s], 0.0)
        top = top - col * line
        hs = [None] * 8
        for k in range(s + 1, 8):
            hs[k] = c[k][s : s + 1, :] * inv
            c[k] = c[k] - col * hs[k]
        lines.append(line)
        steps.append(hs)
    top = top * lax.rsqrt(pivots)
    top = jnp.where((lane < 8) | (lane >= n - 8 * g), top, 0.0)
    out[pl.ds(pl.multiple_of(g * 8, 8), 8), :] = pltpu.roll(top, 8 * g, 1)
    rest = []
    for r in range(1, 16):
        cr = [jnp.broadcast_to(m[8 * r : 8 * r + 8, 8 + k : 9 + k], (8, n)) for k in range(8)]
        acc = jnp.where(lane < 8, 0.0, turned[8 * r : 8 * r + 8])
        for s in range(8):
            for k in range(s + 1, 8):
                cr[k] = cr[k] - cr[s] * steps[s][k]
            acc = acc - cr[s] * lines[s]
        rest.append(acc)
    return jnp.concatenate(rest + [jnp.zeros((8, n), F32)], 0)


def dot(a, b):
    return jnp.dot(a, b, precision=HIGHEST, preferred_element_type=F32)


def dot_nt(a, b):
    return lax.dot_general(a, b, NT, precision=HIGHEST, preferred_element_type=F32)


def factor_items(gram, inv, turning, done, blocks, pieces):
    items = []
    size = blocks * 128
    for j in range(blocks):
        lo, hi = j * 128, (j + 1) * 128
        for p in range(pieces):

            def pivots(p=p, lo=lo, hi=hi):
                m = pltpu.roll(gram[lo:hi, lo:hi], 8, 1) if p == 0 else turning[...]
                step = 16 // pieces
                m = lax.fori_loop(p * step, (p + 1) * step, lambda g, m: eight(g, m, done), m)
                if p < pieces - 1:
                    turning[...] = m

            items.append(pivots)

        def rows(lo=lo, hi=hi):
            w = done[...]
            inv[lo:hi, lo:hi] = w
            if lo:
                inv[lo:hi, 0:lo] = dot(w, inv[lo:hi, 0:lo])
            if hi < size:
                gram[hi:, lo:hi] = dot_nt(gram[hi:, lo:hi], w)

        items.append(rows)
        if hi < size:

            def below(lo=lo, hi=hi):
                factor = gram[hi:, lo:hi]
                for k in range(hi, size, 128):
                    gram[k:, k : k + 128] -= dot_nt(factor[k - hi :], factor[k - hi : k - hi + 128])
                inv[hi:, 0:hi] -= dot(factor, inv[lo:hi, 0:hi])

            items.append(below)
    return items


def comm_kernel(
    x, v, old, panel_o, oldall, pall, winv, bout, cout,
    xt, vsend, vg, part, bufr, bufl, first,
    apart, asib, ash, apl, aout, gram, turning, done,
    bpart, bsib, bs, br, bz, bsh, bfin,
    cpart, csib, cs, cr, cz, csh, cfin,
    ag_s, ag_r, fw_s, fw_r, rs_s, rs_r, og_s, og_r, pg_s, pg_r, az_s, az_r,
    a_s, a_r, b_s, b_r, c_s, c_r,
):
    row = lax.axis_index("row")
    z = lax.axis_index("col")
    chip = row // 2
    core = row % 2
    sib = (chip * 2 + 1 - core, z)
    right = (row, (z + 1) % 16)
    left = (row, (z + 15) % 16)

    def plane(d):
        y = (chip // 4 + d // 4) % 4
        w = (chip % 4 + d % 4) % 4
        return y * 4 + w

    def remote(src, dst, ssem, rsem, target):
        return pltpu.make_async_remote_copy(
            src_ref=src, dst_ref=dst, send_sem=ssem, recv_sem=rsem, device_id=target, device_id_type=MESH
        )

    barrier = pltpu.get_barrier_semaphore()

    @pl.loop(1, 16)
    def _(d):
        pl.semaphore_signal(barrier, inc=1, device_id=(plane(d) * 2 + core, z), device_id_type=MESH)
        pl.semaphore_signal(barrier, inc=1, device_id=(row, (z + d) % 16), device_id_type=MESH)

    pl.semaphore_signal(barrier, inc=1, device_id=sib, device_id_type=MESH)
    vsend[0] = v[...]
    pl.semaphore_wait(barrier, 31)

    def plane_push(src, dst, ssem, rsem):
        @pl.loop(1, 16)
        def _(d):
            remote(src, dst, ssem, rsem, (plane(d) * 2 + core, z)).start()

    def bulk(ref, ssem, rsem):
        return remote(ref.at[pl.ds(0, 15)], ref.at[pl.ds(0, 15)], ssem, rsem, sib)

    def gather_start(m):
        plane_push(vsend.at[m], vg.at[m, core * 16 + chip], ag_s.at[m], ag_r.at[m])
        vg[m, core * 16 + chip] = vsend[m]

    def product(m, half, add):
        rhs = vg[m, pl.ds(half * 16, 16)].reshape(1024, 256)
        for rb in range(2):
            lhs = xt[pl.ds(rb * 512, 512), pl.ds(pl.multiple_of(half * 1024, 1024), 1024)]
            res = jnp.dot(lhs, rhs, preferred_element_type=F32).reshape(8, 64, 256)
            if add:
                part[m, pl.ds(rb * 8, 8)] += res
            else:
                part[m, pl.ds(rb * 8, 8)] = res

    def gather_product(m):
        wait = bulk(vg.at[m], ag_s.at[m], ag_r.at[m])
        wait.wait_recv()
        span = vg.at[m, pl.ds(core * 16, 16)]
        forward = remote(span, span, fw_s.at[m], fw_r.at[m], sib)
        forward.start()
        product(m, core, False)
        forward.wait_recv()
        product(m, 1 - core, True)
        wait.wait_send()
        forward.wait_send()

    def rs_copy(m, way, s):
        buf, to = (bufr, right) if way == 0 else (bufl, left)
        dest = (z + 8 - s) % 16 if way == 0 else (z + 9 + s) % 16
        return remote(part.at[m, dest], buf.at[m, s], rs_s.at[m, way, s], rs_r.at[m, way, s], to), dest

    def reduce_scatter(m, hook):
        for way in (0, 1):
            rs_copy(m, way, 0)[0].start()
        hook(0)
        for s in range(1, 8):
            for way in (0, 1):
                if way == 1 and s == 7:
                    continue
                rs_copy(m, way, s - 1)[0].wait_recv()
                copy, dest = rs_copy(m, way, s)
                buf = bufr if way == 0 else bufl
                part[m, dest] += buf[m, s - 1]
                copy.start()
            hook(s)
        rs_copy(m, 1, 6)[0].wait_recv()
        rs_copy(m, 0, 7)[0].wait_recv()
        res = part[m, z] + bufr[m, 7] + bufl[m, 6]
        for s in range(8):
            rs_copy(m, 0, s)[0].wait_send()
            if s < 7:
                rs_copy(m, 1, s)[0].wait_send()
        return res

    def ring(own, blocks, ssem, rsem):
        def copy(way, s):
            idx = (z - s + 16) % 16 if way == 0 else (z + s) % 16
            return remote(
                own if s == 0 else blocks.at[idx], blocks.at[idx], ssem.at[way, s], rsem.at[way, s],
                right if way == 0 else left,
            )

        def step(s):
            for way in (0, 1):
                if s > 0 and not (way == 1 and s == 8):
                    copy(way, s - 1).wait_recv()
                if s < 8 and not (way == 1 and s == 7):
                    copy(way, s).start()

        def finish():
            for s in range(8):
                copy(0, s).wait_send()
                if s < 7:
                    copy(1, s).wait_send()

        return step, finish

    def total_of(parts):
        total = parts[0]
        for q in range(1, 16):
            total = total + parts[q]
        return total

    def all_sum(own, other, mine, terms, zterms, share, final, res, ssem, rsem):
        pair = remote(own.at[1 - core], other, ssem.at[0], rsem.at[0], sib)
        spread = bulk(terms, ssem.at[1], rsem.at[1])
        along = bulk(zterms, ssem.at[2], rsem.at[2])
        back = bulk(res.at[core], ssem.at[3], rsem.at[3])
        half = remote(res.at[core], res.at[core], ssem.at[4], rsem.at[4], sib)

        def to_plane():
            pair.wait_recv()
            mine[...] = own[core] + other[...]

            @pl.loop(1, 16)
            def _(d):
                q = plane(d)
                remote(mine.at[q], terms.at[chip], ssem.at[1], rsem.at[1], (q * 2 + core, z)).start()

            terms[chip] = mine[chip]

        def to_column():
            spread.wait_recv()
            share[...] = total_of(terms)

            @pl.loop(1, 16)
            def _(d):
                remote(share, zterms.at[z], ssem.at[2], rsem.at[2], (row, (z + d) % 16)).start()

            zterms[z] = share[...]

        def to_back():
            along.wait_recv()
            final[...] = total_of(zterms) * (1.0 / NSTATE)
            plane_push(final, res.at[core, chip], ssem.at[3], rsem.at[3])
            res[core, chip] = final[...]

        def to_half():
            back.wait_recv()
            half.start()

        def finish():
            half.wait_recv()
            for copy in (pair, spread, along, back, half):
                copy.wait_send()

        return pair.start, to_plane, to_column, to_back, to_half, finish

    gather_start(0)
    old_step, old_finish = ring(old, oldall, og_s, og_r)
    old_step(0)
    oldall[z] = old[...]

    @pl.loop(0, 16)
    def _(t):
        a = (t % 8) * 4 + t // 8
        both = jnp.concatenate([x[a, 0], x[a + 2, 0]], 0)
        xt[:, pl.ds(pl.multiple_of(t * 128, 128), 128)] = both.T

    old_step(1)
    old_step(2)
    gather_product(0)

    a_pair = remote(apart.at[1 - core], asib, a_s.at[0], a_r.at[0], sib)

    def hook0(s):
        if 1 <= s <= 6:
            old_step(2 + s)
        if s == 7:
            every = oldall[...].reshape(512, 1024)
            share = lax.dot_general(old[...], every, NT, preferred_element_type=F32)
            apart[...] = share.reshape(2, 16, 512)
            a_pair.start()

    first_full = reduce_scatter(0, hook0)
    first[...] = first_full
    vsend[1] = first_full.astype(BF)
    gather_start(1)
    old_finish()
    a_pair.wait_recv()
    ash[...] = apart[core] + asib[...]
    plane_push(ash, apl.at[chip], a_s.at[1], a_r.at[1])
    apl[chip] = ash[...]
    a_spread = bulk(apl, a_s.at[1], a_r.at[1])
    a_step, a_finish = ring(aout.at[core, z], aout.at[core], az_s, az_r)
    a_half = remote(aout.at[core], aout.at[core], a_s.at[2], a_r.at[2], sib)
    winv[...] = jnp.zeros((512, 512), F32)
    side = z % 2
    own_rows = lax.broadcasted_iota(jnp.int32, (128, 256), 0) // 64 == side

    def own_states(a):
        return jnp.where(own_rows, jnp.concatenate([a, a], 0), 0.0)

    gather_product(1)

    def hook1(s):
        if s == 1:
            a_spread.wait_recv()
            aout[core, z] = total_of(apl) * (1.0 / NSTATE)
        if s >= 1:
            a_step(s - 1)

    second = reduce_scatter(1, hook1)
    vsend[2] = second.astype(BF)
    gather_start(2)
    a_step(7)
    a_step(8)
    a_half.start()
    gather_product(2)

    def assemble():
        a_half.wait_recv()

        @pl.loop(0, 16)
        def _(c):
            for h in range(2):
                gram[pl.ds(pl.multiple_of(c * 32 + h * 16, 16), 16), :] = aout[h, c]

    items = [assemble] + factor_items(gram, winv, turning, done, 4, 4)

    def work(count):
        for _ in range(min(count, len(items))):
            items.pop(0)()

    b_start, b_plane, b_column, b_back, b_half, b_finish = all_sum(
        bpart, bsib, bs, br, bz, bsh, bfin, bout, b_s, b_r
    )

    def hook2(s):
        if s == 0:
            every = oldall[...].reshape(512, 1024)
            window = oldall[:, :, pl.ds(pl.multiple_of((z // 2) * 128, 128), 128)].reshape(512, 128)
            cross = jnp.zeros((512, 256), F32)
            for t in split3(part[2].reshape(1024, 256) * -0.5):
                cross = cross + jnp.dot(every, t, preferred_element_type=F32)
            for t in split3(own_states(first[...] * 1.5)):
                cross = cross + jnp.dot(window, t, preferred_element_type=F32)
            bpart[...] = cross.reshape(2, 16, 16, 256)
            b_start()
        if s == 1:
            b_plane()
        if s == 5:
            b_column()
        if s in (2, 3, 4, 6, 7):
            work(1)

    third = reduce_scatter(2, hook2)
    panel = 1.5 * first[...] - 0.5 * third
    panel_o[...] = panel
    p_step, p_finish = ring(panel_o, pall, pg_s, pg_r)
    p_step(0)
    pall[z] = panel
    turned = panel.T
    cpart[...] = dot_nt(turned, turned).reshape(2, 16, 8, 256)
    c_start, c_plane, c_column, c_back, c_half, c_finish = all_sum(
        cpart, csib, cs, cr, cz, csh, cfin, cout, c_s, c_r
    )
    c_start()
    work(1)
    c_plane()
    p_step(1)
    work(2)
    b_back()
    p_step(2)
    work(2)
    c_column()
    p_step(3)
    work(2)
    p_step(4)
    work(2)
    b_half()
    p_step(5)
    work(2)
    c_back()
    p_step(6)
    work(2)
    p_step(7)
    work(2)
    c_half()
    p_step(8)
    work(100)
    p_finish()
    a_finish()
    for copy in (a_pair, a_spread, a_half):
        copy.wait_send()
    b_finish()
    c_finish()


def basis_kernel(winv, bout, cout, oldall, pall, basis_o, gram, inv, turning, done, full):
    z = lax.axis_index("col")
    first = winv[...]
    cross = bout[...].reshape(512, 256).T
    lower = dot_nt(cross, first)
    gram[...] = cout[...].reshape(256, 256) - dot_nt(lower, lower)
    inv[...] = jnp.zeros((256, 256), F32)
    for item in factor_items(gram, inv, turning, done, 2, 1):
        item()
    last = inv[...]
    full[0:512, 0:512] = first
    full[0:512, 512:768] = jnp.zeros((512, 256), F32)
    full[512:768, 0:512] = -dot(last, dot(lower, first))
    full[512:768, 512:768] = last
    mine = full[pl.ds(pl.multiple_of(z * 48, 16), 48), :]
    every = oldall[...].reshape(512, 1024)
    res = dot_nt(mine[:, 512:], pall[...].reshape(1024, 256))
    for t in split3(mine[:, :512]):
        res = res + jnp.dot(t, every, preferred_element_type=F32)
    basis_o[...] = res


def body(iterate_t, vectors, old_factor_t):
    vm = pl.BlockSpec(memory_space=pltpu.VMEM)
    dma = pltpu.SemaphoreType.DMA
    out = jax.ShapeDtypeStruct

    def f32(*shape):
        return pltpu.VMEM(shape, F32)

    panel, oldall, pall, winv, bout, cout = pl.pallas_call(
        comm_kernel,
        out_shape=(
            out((64, 256), F32),
            out((16, 32, 1024), BF),
            out((16, 64, 256), F32),
            out((512, 512), F32),
            out((2, 16, 16, 256), F32),
            out((2, 16, 8, 256), F32),
        ),
        in_specs=[vm] * 3,
        out_specs=(vm,) * 6,
        scratch_shapes=[
            pltpu.VMEM((1024, 2048), BF),
            pltpu.VMEM((3, 64, 256), BF),
            pltpu.VMEM((3, 32, 64, 256), BF),
            f32(3, 16, 64, 256), f32(3, 8, 64, 256), f32(3, 7, 64, 256), f32(64, 256),
            f32(2, 16, 512), f32(16, 512), f32(16, 512), f32(16, 16, 512), f32(2, 16, 16, 512),
            f32(512, 512), f32(128, 128), f32(128, 128),
            f32(2, 16, 16, 256), f32(16, 16, 256), f32(16, 16, 256), f32(16, 16, 256), f32(16, 16, 256),
            f32(16, 256), f32(16, 256),
            f32(2, 16, 8, 256), f32(16, 8, 256), f32(16, 8, 256), f32(16, 8, 256), f32(16, 8, 256),
            f32(8, 256), f32(8, 256),
            dma((3,)), dma((3,)), dma((3,)), dma((3,)),
            dma((3, 2, 8)), dma((3, 2, 8)),
            dma((2, 8)), dma((2, 8)),
            dma((2, 8)), dma((2, 8)),
            dma((2, 8)), dma((2, 8)),
            dma((3,)), dma((3,)),
            dma((5,)), dma((5,)), dma((5,)), dma((5,)),
        ],
        compiler_params=pltpu.CompilerParams(
            collective_id=0, has_side_effects=True, vmem_limit_bytes=48 << 20
        ),
        name="sign_step",
    )(iterate_t, vectors, old_factor_t)
    basis = pl.pallas_call(
        basis_kernel,
        out_shape=out((48, 1024), F32),
        in_specs=[vm] * 5,
        out_specs=vm,
        scratch_shapes=[f32(256, 256), f32(256, 256), f32(128, 128), f32(128, 128), f32(768, 768)],
        compiler_params=pltpu.CompilerParams(vmem_limit_bytes=48 << 20),
        name="recompress",
    )(winv, bout, cout, oldall, pall)
    return panel, basis


def solution(mesh):
    return jax.shard_map(
        body,
        mesh=mesh,
        in_specs=(P(None, "col", None, "row"), P(("row", "col"), None), P("col", "row")),
        out_specs=(P(("row", "col"), None), P("col", "row")),
        check_vma=False,
    )
```

```python
import functools

import jax
import jax.numpy as jnp
from jax import lax
from jax.experimental import pallas as pl
from jax.experimental.pallas import tpu as pltpu
from jax.sharding import PartitionSpec as P

NSTATE = 32768
MESH = pl.DeviceIdType.MESH
HIGHEST = lax.Precision.HIGHEST
BF = jnp.bfloat16
F32 = jnp.float32
NT = (((1,), (1,)), ((), ()))


def split3(a):
    hi = a.astype(BF)
    rest = a - hi.astype(F32)
    mid = rest.astype(BF)
    low = (rest - mid.astype(F32)).astype(BF)
    return hi, mid, low


def eight(g, m, out):
    n = 128
    sub = lax.broadcasted_iota(jnp.int32, (8, n), 0)
    lane = lax.broadcasted_iota(jnp.int32, (8, n), 1)
    c = [jnp.broadcast_to(m[:8, 8 + k : 9 + k], (8, n)) for k in range(8)]
    turned = pltpu.roll(m, n - 8, 1)
    top = jnp.where(lane < 8, jnp.where(lane == sub, 1.0, 0.0), turned[:8])
    lines, steps, pivots = [], [], c[0]
    for s in range(8):
        if s:
            pivots = jnp.where(sub == s, c[s], pivots)
        inv = 1.0 / c[s][s : s + 1, :]
        line = top[s : s + 1, :] * inv
        col = jnp.where(sub > s, c[s], 0.0)
        top = top - col * line
        hs = [None] * 8
        for k in range(s + 1, 8):
            hs[k] = c[k][s : s + 1, :] * inv
            c[k] = c[k] - col * hs[k]
        lines.append(line)
        steps.append(hs)
    top = top * lax.rsqrt(pivots)
    top = jnp.where((lane < 8) | (lane >= n - 8 * g), top, 0.0)
    out[pl.ds(pl.multiple_of(g * 8, 8), 8), :] = pltpu.roll(top, 8 * g, 1)
    rest = []
    for r in range(1, 16):
        cr = [jnp.broadcast_to(m[8 * r : 8 * r + 8, 8 + k : 9 + k], (8, n)) for k in range(8)]
        acc = jnp.where(lane < 8, 0.0, turned[8 * r : 8 * r + 8])
        for s in range(8):
            for k in range(s + 1, 8):
                cr[k] = cr[k] - cr[s] * steps[s][k]
            acc = acc - cr[s] * lines[s]
        rest.append(acc)
    return jnp.concatenate(rest + [jnp.zeros((8, n), F32)], 0)


def dot(a, b):
    return jnp.dot(a, b, precision=HIGHEST, preferred_element_type=F32)


def dot_nt(a, b):
    return lax.dot_general(a, b, NT, precision=HIGHEST, preferred_element_type=F32)


def factor_items(gram, inv, turning, done, blocks, pieces):
    items = []
    size = blocks * 128
    for j in range(blocks):
        lo, hi = j * 128, (j + 1) * 128
        for p in range(pieces):

            def pivots(p=p, lo=lo, hi=hi):
                m = pltpu.roll(gram[lo:hi, lo:hi], 8, 1) if p == 0 else turning[...]
                step = 16 // pieces
                m = lax.fori_loop(p * step, (p + 1) * step, lambda g, m: eight(g, m, done), m)
                if p < pieces - 1:
                    turning[...] = m

            items.append(pivots)

        def rows(lo=lo, hi=hi):
            w = done[...]
            inv[lo:hi, lo:hi] = w
            if lo:
                inv[lo:hi, 0:lo] = dot(w, inv[lo:hi, 0:lo])
            if hi < size:
                gram[hi:size, lo:hi] = dot_nt(gram[hi:size, lo:hi], w)

        items.append(rows)
        if hi < size:

            def below(lo=lo, hi=hi):
                factor = gram[hi:size, lo:hi]
                for k in range(hi, size, 128):
                    gram[k:size, k : k + 128] -= dot_nt(factor[k - hi :], factor[k - hi : k - hi + 128])
                inv[hi:size, 0:hi] -= dot(factor, inv[lo:hi, 0:hi])

            items.append(below)
    return items


def comm_kernel(
    x, v, old, panel_o, basis_o,
    xs, xt, vsend, vg, part, meet, hub_sum, landed, first, oldall, pall,
    apart, asib, ash, apl, aout, gram, turning, done, winv,
    bsplit, bpart, bsib, bs, br, bz, bsh, bfin, bout,
    cpart, csib, cs, cr, cz, csh, cfin, cout,
    lower, onto, square, gram2, inv2, upper, tmat, x_s,
    ag_s, ag_r, fw_s, fw_r, rs_s, rs_r, og_s, og_r, pg_s, pg_r, az_s, az_r,
    a_s, a_r, b_s, b_r, c_s, c_r,
):
    row = lax.axis_index("row")
    z = lax.axis_index("col")
    chip = row // 2
    core = row % 2
    sib = (chip * 2 + 1 - core, z)
    right = (row, (z + 1) % 16)
    left = (row, (z + 15) % 16)

    def plane(d):
        y = (chip // 4 + d // 4) % 4
        w = (chip % 4 + d % 4) % 4
        return y * 4 + w

    def remote(src, dst, ssem, rsem, target):
        return pltpu.make_async_remote_copy(
            src_ref=src, dst_ref=dst, send_sem=ssem, recv_sem=rsem, device_id=target, device_id_type=MESH
        )

    loads = [
        pltpu.make_async_copy(x.at[pl.ds(8 * q, 8), 0], xs.at[pl.ds(8 * q, 8)], x_s.at[q]) for q in range(4)
    ]
    for load in loads:
        load.start()
    barrier = pltpu.get_barrier_semaphore()

    @pl.loop(1, 16)
    def _(d):
        pl.semaphore_signal(barrier, inc=1, device_id=(plane(d) * 2 + core, z), device_id_type=MESH)
        pl.semaphore_signal(barrier, inc=1, device_id=(row, (z + d) % 16), device_id_type=MESH)

    pl.semaphore_signal(barrier, inc=1, device_id=sib, device_id_type=MESH)
    vsend[0] = v[...]

    for q in range(4):
        loads[q].wait()

        @pl.loop(0, 4)
        def _(u):
            a = 8 * q + (u // 2) * 4 + u % 2
            at = ((u % 2) * 8 + 2 * q + u // 2) * 128
            both = jnp.concatenate([xs[a], xs[a + 2]], 0)
            xt[:, pl.ds(pl.multiple_of(at, 128), 128)] = both.T

    pl.semaphore_wait(barrier, 31)

    def plane_push(src, dst, ssem, rsem):
        @pl.loop(1, 16)
        def _(d):
            remote(src, dst, ssem, rsem, (plane(d) * 2 + core, z)).start()

    def bulk(ref, ssem, rsem):
        return remote(ref.at[pl.ds(0, 15)], ref.at[pl.ds(0, 15)], ssem, rsem, sib)

    def gather_start(m):
        plane_push(vsend.at[m], vg.at[m, core * 16 + chip], ag_s.at[m], ag_r.at[m])
        vg[m, core * 16 + chip] = vsend[m]

    def product(m, half, add):
        rhs = vg[m, pl.ds(half * 16, 16)].reshape(1024, 256)
        for rb in range(2):
            lhs = xt[pl.ds(rb * 512, 512), pl.ds(pl.multiple_of(half * 1024, 1024), 1024)]
            res = jnp.dot(lhs, rhs, preferred_element_type=F32).reshape(8, 64, 256)
            if add:
                part[m, pl.ds(rb * 8, 8)] += res
            else:
                part[m, pl.ds(rb * 8, 8)] = res

    def gather_product(m):
        wait = bulk(vg.at[m], ag_s.at[m], ag_r.at[m])
        wait.wait_recv()
        span = vg.at[m, pl.ds(core * 16, 16)]
        forward = remote(span, span, fw_s.at[m], fw_r.at[m], sib)
        forward.start()
        product(m, core, False)
        forward.wait_recv()
        product(m, 1 - core, True)
        wait.wait_send()
        forward.wait_send()

    def at(d):
        return (z + 16 + d) % 16

    def flight(m, slot, hub, dest, sem):
        return remote(part.at[m, at(dest)], meet.at[m, slot], rs_s.at[m, 0], rs_r.at[m, sem], (row, at(hub)))

    def reduce_scatter(m, early, late):
        for i, d in enumerate((3, 2, -2, 1, -1)):
            flight(m, i, -d, -d - 5, 0).start()
        for i, d in enumerate((2, -2, 1, -1)):
            flight(m, 5 + i, -d, -d + 5, 1).start()
        for i, d in enumerate((2, -2, 1, -1)):
            flight(m, 9 + i, -d, -d, 2).start()

        def met(first, count, sem):
            span = meet.at[m, pl.ds(first, count)]
            remote(span, span, rs_s.at[m, 0], rs_r.at[m, sem], sib).wait_recv()
            total = meet[m, first]
            for k in range(first + 1, first + count):
                total = total + meet[m, k]
            return total

        early()
        onward = []
        for k, (first, count, dest) in enumerate(((0, 5, -5), (5, 4, 5))):
            hub_sum[m, k] = part[m, at(dest)] + met(first, count, k)
            copy = remote(
                hub_sum.at[m, k], landed.at[m, k], rs_s.at[m, 1 + k], rs_r.at[m, 3 + k], (row, at(dest))
            )
            copy.start()
            onward.append(copy)
        near = part[m, z] + met(9, 4, 2)
        late()
        for copy in onward:
            copy.wait_recv()
        res = near + (landed[m, 0] + landed[m, 1])
        span = meet.at[m, pl.ds(0, 13)]
        remote(span, span, rs_s.at[m, 0], rs_r.at[m, 0], sib).wait_send()
        for copy in onward:
            copy.wait_send()
        return res

    def ring(own, blocks, ssem, rsem):
        def copy(way, s):
            idx = (z - s + 16) % 16 if way == 0 else (z + s) % 16
            return remote(
                own if s == 0 else blocks.at[idx], blocks.at[idx], ssem.at[way, s], rsem.at[way, s],
                right if way == 0 else left,
            )

        def step(s):
            for way in (0, 1):
                if s > 0 and not (way == 1 and s == 8):
                    copy(way, s - 1).wait_recv()
                if s < 8 and not (way == 1 and s == 7):
                    copy(way, s).start()

        def finish():
            for s in range(8):
                copy(0, s).wait_send()
                if s < 7:
                    copy(1, s).wait_send()

        return step, finish

    def total_of(parts):
        total = parts[0]
        for q in range(1, 16):
            total = total + parts[q]
        return total

    def all_sum(own, other, mine, terms, zterms, share, final, res, ssem, rsem):
        pair = remote(own.at[1 - core], other, ssem.at[0], rsem.at[0], sib)
        spread = bulk(terms, ssem.at[1], rsem.at[1])
        along = bulk(zterms, ssem.at[2], rsem.at[2])
        back = bulk(res.at[core], ssem.at[3], rsem.at[3])
        half = remote(res.at[core], res.at[core], ssem.at[4], rsem.at[4], sib)

        def to_plane():
            pair.wait_recv()
            mine[...] = own[core] + other[...]

            @pl.loop(1, 16)
            def _(d):
                q = plane(d)
                remote(mine.at[q], terms.at[chip], ssem.at[1], rsem.at[1], (q * 2 + core, z)).start()

            terms[chip] = mine[chip]

        def to_column():
            spread.wait_recv()
            share[...] = total_of(terms)

            @pl.loop(1, 16)
            def _(d):
                remote(share, zterms.at[z], ssem.at[2], rsem.at[2], (row, (z + d) % 16)).start()

            zterms[z] = share[...]

        def to_back():
            along.wait_recv()
            final[...] = total_of(zterms) * (1.0 / NSTATE)
            plane_push(final, res.at[core, chip], ssem.at[3], rsem.at[3])
            res[core, chip] = final[...]

        def to_half():
            back.wait_recv()
            half.start()

        def finish():
            for copy in (pair, spread, along, back, half):
                copy.wait_send()

        return pair.start, to_plane, to_column, to_back, to_half, half.wait_recv, finish

    gather_start(0)
    old_step, old_finish = ring(old, oldall, og_s, og_r)
    old_step(0)
    oldall[z] = old[...]

    old_step(1)
    old_step(2)
    old_step(3)
    gather_product(0)

    a_pair = remote(apart.at[1 - core], asib, a_s.at[0], a_r.at[0], sib)
    a_spread = bulk(apl, a_s.at[1], a_r.at[1])

    def early0():
        for s in (4, 5, 6):
            old_step(s)

    def late0():
        old_step(7)
        old_step(8)
        every = oldall[...].reshape(512, 1024)
        share = lax.dot_general(old[...], every, NT, preferred_element_type=F32)
        apart[...] = share.reshape(2, 16, 512)
        a_pair.start()

    first_full = reduce_scatter(0, early0, late0)
    first[...] = first_full
    vsend[1] = first_full.astype(BF)
    gather_start(1)
    a_pair.wait_recv()
    ash[...] = apart[core] + asib[...]
    plane_push(ash, apl.at[chip], a_s.at[1], a_r.at[1])
    apl[chip] = ash[...]
    old_finish()
    a_step, a_finish = ring(aout.at[core, z], aout.at[core], az_s, az_r)
    a_half = remote(aout.at[core], aout.at[core], a_s.at[2], a_r.at[2], sib)
    winv[...] = jnp.zeros((768, 512), F32)
    upper[...] = jnp.zeros((768, 256), F32)
    inv2[...] = jnp.zeros((256, 256), F32)
    side = z % 2
    own_rows = lax.broadcasted_iota(jnp.int32, (128, 256), 0) // 64 == side

    def own_states(a):
        return jnp.where(own_rows, jnp.concatenate([a, a], 0), 0.0)

    a_spread.wait_recv()
    aout[core, z] = total_of(apl) * (1.0 / NSTATE)
    a_step(0)
    a_step(1)
    gather_product(1)

    def early1():
        for s in (2, 3, 4):
            a_step(s)

    def late1():
        for s in (5, 6, 7):
            a_step(s)

    second = reduce_scatter(1, early1, late1)
    vsend[2] = second.astype(BF)
    gather_start(2)
    a_step(8)
    a_half.start()

    def assemble():
        a_half.wait_recv()

        @pl.loop(0, 16)
        def _(c):
            for h in range(2):
                gram[pl.ds(pl.multiple_of(c * 32 + h * 16, 16), 16), :] = aout[h, c]

    items = [assemble] + factor_items(gram, winv, turning, done, 4, 4)

    def work(count):
        for _ in range(min(count, len(items))):
            items.pop(0)()

    work(6)
    gather_product(2)
    b_start, b_plane, b_column, b_back, b_half, b_ready, b_finish = all_sum(
        bpart, bsib, bs, br, bz, bsh, bfin, bout, b_s, b_r
    )

    def every_old():
        return oldall[...].reshape(512, 1024)

    def early2():
        for t, piece in enumerate(split3(part[2].reshape(1024, 256) * -0.5)):
            bsplit[t] = piece
        cross = jnp.zeros((512, 256), F32)
        for t in range(3):
            cross = cross + jnp.dot(every_old(), bsplit[t], preferred_element_type=F32)
        window = oldall[:, :, pl.ds(pl.multiple_of((z // 2) * 128, 128), 128)].reshape(512, 128)
        for t in split3(own_states(first[...] * 1.5)):
            cross = cross + jnp.dot(window, t, preferred_element_type=F32)
        bpart[...] = cross.reshape(2, 16, 16, 256)
        b_start()
        work(1)

    def late2():
        b_plane()
        work(4)

    third = reduce_scatter(2, early2, late2)
    panel = 1.5 * first[...] - 0.5 * third
    panel_o[...] = panel
    p_step, p_finish = ring(panel_o, pall, pg_s, pg_r)
    turned = panel.T
    cpart[...] = dot_nt(turned, turned).reshape(2, 16, 8, 256)
    c_start, c_plane, c_column, c_back, c_half, c_ready, c_finish = all_sum(
        cpart, csib, cs, cr, cz, csh, cfin, cout, c_s, c_r
    )
    c_start()
    p_step(0)
    pall[z] = panel
    c_plane()
    b_column()

    def to_lower():
        b_ready()
        lower[...] = dot_nt(bout[...].reshape(512, 256).T, winv[0:512, :])

    def to_square():
        square[...] = dot_nt(lower[...], lower[...])

    def to_onto():
        onto[...] = dot(lower[...], winv[0:512, :])

    def to_old_rows():
        res = jnp.zeros((48, 1024), F32)
        for t in split3(winv[pl.ds(pl.multiple_of(z * 48, 16), 48), :]):
            res = res + jnp.dot(t, every_old(), preferred_element_type=F32)
        basis_o[...] = res

    def to_rest():
        res = pall[...].reshape(1024, 256).T
        for t in split3(onto[...]):
            res = res - jnp.dot(t, every_old(), preferred_element_type=F32)
        tmat[...] = res

    items.extend([to_lower, to_square, to_onto, to_old_rows])
    p_step(1)
    work(3)
    c_column()
    b_back()
    p_step(2)
    work(2)
    p_step(3)
    work(2)
    b_half()
    p_step(4)
    work(2)
    c_back()
    p_step(5)
    work(2)
    p_step(6)
    work(1)
    c_half()
    p_step(7)
    work(100)
    p_step(8)
    to_rest()
    c_ready()
    gram2[...] = cout[...].reshape(256, 256) - square[...]
    for item in factor_items(gram2, inv2, turning, done, 2, 1):
        item()
    upper[512:768, :] = inv2[...]
    basis_o[...] += dot(upper[pl.ds(pl.multiple_of(z * 48, 16), 48), :], tmat[...])
    p_finish()
    a_finish()
    for copy in (a_pair, a_spread, a_half):
        copy.wait_send()
    b_finish()
    c_finish()


def body(iterate_t, vectors, old_factor_t):
    vm = pl.BlockSpec(memory_space=pltpu.VMEM)
    dma = pltpu.SemaphoreType.DMA
    out = jax.ShapeDtypeStruct

    def f32(*shape):
        return pltpu.VMEM(shape, F32)

    return pl.pallas_call(
        comm_kernel,
        out_shape=(out((64, 256), F32), out((48, 1024), F32)),
        in_specs=[pl.BlockSpec(memory_space=pl.ANY), vm, vm],
        out_specs=(vm, vm),
        scratch_shapes=[
            pltpu.VMEM((32, 64, 1024), BF),
            pltpu.VMEM((1024, 2048), BF),
            pltpu.VMEM((3, 64, 256), BF),
            pltpu.VMEM((3, 32, 64, 256), BF),
            f32(3, 16, 64, 256), f32(3, 13, 64, 256), f32(3, 2, 64, 256), f32(3, 2, 64, 256), f32(64, 256),
            pltpu.VMEM((16, 32, 1024), BF), f32(16, 64, 256),
            f32(2, 16, 512), f32(16, 512), f32(16, 512), f32(16, 16, 512), f32(2, 16, 16, 512),
            f32(512, 512), f32(128, 128), f32(128, 128), f32(768, 512),
            pltpu.VMEM((3, 1024, 256), BF),
            f32(2, 16, 16, 256), f32(16, 16, 256), f32(16, 16, 256), f32(16, 16, 256), f32(16, 16, 256),
            f32(16, 256), f32(16, 256), f32(2, 16, 16, 256),
            f32(2, 16, 8, 256), f32(16, 8, 256), f32(16, 8, 256), f32(16, 8, 256), f32(16, 8, 256),
            f32(8, 256), f32(8, 256), f32(2, 16, 8, 256),
            f32(256, 512), f32(256, 512), f32(256, 256), f32(256, 256), f32(256, 256), f32(768, 256),
            f32(256, 1024), dma((4,)),
            dma((3,)), dma((3,)), dma((3,)), dma((3,)),
            dma((3, 3)), dma((3, 5)),
            dma((2, 8)), dma((2, 8)),
            dma((2, 8)), dma((2, 8)),
            dma((2, 8)), dma((2, 8)),
            dma((3,)), dma((3,)),
            dma((5,)), dma((5,)), dma((5,)), dma((5,)),
        ],
        compiler_params=pltpu.CompilerParams(
            collective_id=0, has_side_effects=True, vmem_limit_bytes=56 << 20
        ),
        name="sign_step",
    )(iterate_t, vectors, old_factor_t)


def solution(mesh):
    return jax.shard_map(
        body,
        mesh=mesh,
        in_specs=(P(None, "col", None, "row"), P(("row", "col"), None), P("col", "row")),
        out_specs=(P(("row", "col"), None), P("col", "row")),
        check_vma=False,
    )
```

```python
import functools

import jax
import jax.numpy as jnp
from jax import lax
from jax.experimental import pallas as pl
from jax.experimental.pallas import tpu as pltpu
from jax.sharding import PartitionSpec as P

NSTATE = 32768
MESH = pl.DeviceIdType.MESH
HIGHEST = lax.Precision.HIGHEST
BF = jnp.bfloat16
F32 = jnp.float32
NT = (((1,), (1,)), ((), ()))


def split3(a):
    hi = a.astype(BF)
    rest = a - hi.astype(F32)
    mid = rest.astype(BF)
    low = (rest - mid.astype(F32)).astype(BF)
    return hi, mid, low


def eight(g, m, out):
    n = 128
    sub = lax.broadcasted_iota(jnp.int32, (8, n), 0)
    lane = lax.broadcasted_iota(jnp.int32, (8, n), 1)
    c = [jnp.broadcast_to(m[:8, 8 + k : 9 + k], (8, n)) for k in range(8)]
    turned = pltpu.roll(m, n - 8, 1)
    top = jnp.where(lane < 8, jnp.where(lane == sub, 1.0, 0.0), turned[:8])
    lines, steps, pivots = [], [], c[0]
    for s in range(8):
        if s:
            pivots = jnp.where(sub == s, c[s], pivots)
        inv = 1.0 / c[s][s : s + 1, :]
        line = top[s : s + 1, :] * inv
        col = jnp.where(sub > s, c[s], 0.0)
        top = top - col * line
        hs = [None] * 8
        for k in range(s + 1, 8):
            hs[k] = c[k][s : s + 1, :] * inv
            c[k] = c[k] - col * hs[k]
        lines.append(line)
        steps.append(hs)
    top = top * lax.rsqrt(pivots)
    top = jnp.where((lane < 8) | (lane >= n - 8 * g), top, 0.0)
    out[pl.ds(pl.multiple_of(g * 8, 8), 8), :] = pltpu.roll(top, 8 * g, 1)
    rest = []
    for r in range(1, 16):
        cr = [jnp.broadcast_to(m[8 * r : 8 * r + 8, 8 + k : 9 + k], (8, n)) for k in range(8)]
        acc = jnp.where(lane < 8, 0.0, turned[8 * r : 8 * r + 8])
        for s in range(8):
            for k in range(s + 1, 8):
                cr[k] = cr[k] - cr[s] * steps[s][k]
            acc = acc - cr[s] * lines[s]
        rest.append(acc)
    return jnp.concatenate(rest + [jnp.zeros((8, n), F32)], 0)


def dot(a, b):
    return jnp.dot(a, b, precision=HIGHEST, preferred_element_type=F32)


def dot_nt(a, b):
    return lax.dot_general(a, b, NT, precision=HIGHEST, preferred_element_type=F32)


def factor_items(gram, inv, turning, done, blocks, pieces):
    items = []
    size = blocks * 128
    for j in range(blocks):
        lo, hi = j * 128, (j + 1) * 128
        for p in range(pieces):

            def pivots(p=p, lo=lo, hi=hi):
                m = pltpu.roll(gram[lo:hi, lo:hi], 8, 1) if p == 0 else turning[...]
                step = 16 // pieces
                m = lax.fori_loop(p * step, (p + 1) * step, lambda g, m: eight(g, m, done), m)
                if p < pieces - 1:
                    turning[...] = m

            items.append(pivots)

        def rows(lo=lo, hi=hi):
            w = done[...]
            inv[lo:hi, lo:hi] = w
            if lo:
                inv[lo:hi, 0:lo] = dot(w, inv[lo:hi, 0:lo])
            if hi < size:
                gram[hi:size, lo:hi] = dot_nt(gram[hi:size, lo:hi], w)

        items.append(rows)
        if hi < size:

            def below(lo=lo, hi=hi):
                factor = gram[hi:size, lo:hi]
                for k in range(hi, size, 128):
                    gram[k:size, k : k + 128] -= dot_nt(factor[k - hi :], factor[k - hi : k - hi + 128])
                inv[hi:size, 0:hi] -= dot(factor, inv[lo:hi, 0:hi])

            items.append(below)
    return items


def comm_kernel(
    x, v, old, panel_o, basis_o,
    xs, xt, vsend, vg, part, bufr, bufl, first, oldall, pall,
    apart, asib, ash, apl, afin, aout, gram, turning, done, winv,
    bsplit, bacc, bpart, bsib, bs, br, bz, bsh, bfin, bout,
    cpart, csib, cs, cr, cz, csh, cfin, cout,
    lower, onto, square, gram2, inv2, upper, tmat, x_s,
    ag_s, ag_r, fw_s, fw_r, rs_s, rs_r, og_s, og_r, pg_s, pg_r,
    a_s, a_r, b_s, b_r, c_s, c_r,
):
    row = lax.axis_index("row")
    z = lax.axis_index("col")
    chip = row // 2
    core = row % 2
    sib = (chip * 2 + 1 - core, z)
    right = (row, (z + 1) % 16)
    left = (row, (z + 15) % 16)

    def plane(d):
        y = (chip // 4 + d // 4) % 4
        w = (chip % 4 + d % 4) % 4
        return y * 4 + w

    def remote(src, dst, ssem, rsem, target):
        return pltpu.make_async_remote_copy(
            src_ref=src, dst_ref=dst, send_sem=ssem, recv_sem=rsem, device_id=target, device_id_type=MESH
        )

    loads = [
        pltpu.make_async_copy(x.at[pl.ds(8 * q, 8), 0], xs.at[pl.ds(8 * q, 8)], x_s.at[q]) for q in range(4)
    ]
    for load in loads:
        load.start()
    barrier = pltpu.get_barrier_semaphore()

    @pl.loop(1, 16)
    def _(d):
        pl.semaphore_signal(barrier, inc=1, device_id=(plane(d) * 2 + core, z), device_id_type=MESH)
        pl.semaphore_signal(barrier, inc=1, device_id=(row, (z + d) % 16), device_id_type=MESH)

    pl.semaphore_signal(barrier, inc=1, device_id=sib, device_id_type=MESH)
    vsend[0] = v[...]

    for q in range(4):
        loads[q].wait()

        @pl.loop(0, 4)
        def _(u):
            a = 8 * q + (u // 2) * 4 + u % 2
            at = ((u % 2) * 8 + 2 * q + u // 2) * 128
            both = jnp.concatenate([xs[a], xs[a + 2]], 0)
            xt[:, pl.ds(pl.multiple_of(at, 128), 128)] = both.T

    pl.semaphore_wait(barrier, 31)

    def plane_push(src, dst, ssem, rsem):
        @pl.loop(1, 16)
        def _(d):
            remote(src, dst, ssem, rsem, (plane(d) * 2 + core, z)).start()

    def bulk(ref, ssem, rsem):
        return remote(ref.at[pl.ds(0, 15)], ref.at[pl.ds(0, 15)], ssem, rsem, sib)

    def gather_start(m):
        for d in (10, 9, 11, 6, 14, 2, 8, 5, 7, 13, 15, 1, 3, 4, 12):
            remote(
                vsend.at[m], vg.at[m, core * 16 + chip], ag_s.at[m], ag_r.at[m], (plane(d) * 2 + core, z)
            ).start()
        vg[m, core * 16 + chip] = vsend[m]

    def product(m, half, add):
        rhs = vg[m, pl.ds(half * 16, 16)].reshape(1024, 256)
        for rb in range(2):
            lhs = xt[pl.ds(rb * 512, 512), pl.ds(pl.multiple_of(half * 1024, 1024), 1024)]
            res = jnp.dot(lhs, rhs, preferred_element_type=F32).reshape(8, 64, 256)
            if add:
                part[m, pl.ds(rb * 8, 8)] += res
            else:
                part[m, pl.ds(rb * 8, 8)] = res

    def gather_product(m):
        wait = bulk(vg.at[m], ag_s.at[m], ag_r.at[m])
        wait.wait_recv()
        span = vg.at[m, pl.ds(core * 16, 16)]
        forward = remote(span, span, fw_s.at[m], fw_r.at[m], sib)
        forward.start()
        product(m, core, False)
        forward.wait_recv()
        product(m, 1 - core, True)
        wait.wait_send()
        forward.wait_send()

    def rs_copy(m, way, s, h):
        buf, to = (bufr, right) if way == 0 else (bufl, left)
        dest = (z + 8 - s) % 16 if way == 0 else (z + 9 + s) % 16
        rows = pl.ds(h * 32, 32)
        return remote(
            part.at[m, dest, rows], buf.at[m, s, rows], rs_s.at[m, way, s, h], rs_r.at[m, way, s, h], to
        ), dest

    def reduce_scatter(m, hook):
        for h in (0, 1):
            for way in (0, 1):
                rs_copy(m, way, 0, h)[0].start()
        hook(0)
        for s in range(1, 8):
            for h in (0, 1):
                for way in (0, 1):
                    if way == 1 and s == 7:
                        continue
                    rs_copy(m, way, s - 1, h)[0].wait_recv()
                    copy, dest = rs_copy(m, way, s, h)
                    rows = pl.ds(h * 32, 32)
                    part[m, dest, rows] += (bufr if way == 0 else bufl)[m, s - 1, rows]
                    copy.start()
            hook(s)
        for h in (0, 1):
            rs_copy(m, 1, 6, h)[0].wait_recv()
            rs_copy(m, 0, 7, h)[0].wait_recv()
        res = part[m, z] + bufr[m, 7] + bufl[m, 6]
        for h in (0, 1):
            for s in range(8):
                rs_copy(m, 0, s, h)[0].wait_send()
                if s < 7:
                    rs_copy(m, 1, s, h)[0].wait_send()
        return res

    def ring(own, blocks, ssem, rsem):
        def copy(way, s):
            idx = (z - s + 16) % 16 if way == 0 else (z + s) % 16
            return remote(
                own if s == 0 else blocks.at[idx], blocks.at[idx], ssem.at[way, s], rsem.at[way, s],
                right if way == 0 else left,
            )

        def step(s):
            for way in (0, 1):
                if s > 0 and not (way == 1 and s == 8):
                    copy(way, s - 1).wait_recv()
                if s < 8 and not (way == 1 and s == 7):
                    copy(way, s).start()

        def finish():
            for s in range(8):
                copy(0, s).wait_send()
                if s < 7:
                    copy(1, s).wait_send()

        return step, finish

    def total_of(parts):
        total = parts[0]
        for q in range(1, 16):
            total = total + parts[q]
        return total

    def all_sum(own, other, mine, terms, zterms, share, final, res, ssem, rsem):
        pair = remote(own.at[1 - core], other, ssem.at[0], rsem.at[0], sib)
        spread = bulk(terms, ssem.at[1], rsem.at[1])
        along = None if zterms is None else bulk(zterms, ssem.at[2], rsem.at[2])
        back = bulk(res.at[core], ssem.at[3], rsem.at[3])
        half = remote(res.at[core], res.at[core], ssem.at[4], rsem.at[4], sib)

        def to_plane():
            pair.wait_recv()
            mine[...] = own[core] + other[...]

            @pl.loop(1, 16)
            def _(d):
                q = plane(d)
                remote(mine.at[q], terms.at[chip], ssem.at[1], rsem.at[1], (q * 2 + core, z)).start()

            terms[chip] = mine[chip]

        def to_column():
            spread.wait_recv()
            if along is None:
                final[...] = total_of(terms) * (1.0 / NSTATE)
                send_back()
                return
            share[...] = total_of(terms)

            @pl.loop(1, 16)
            def _(d):
                remote(share, zterms.at[z], ssem.at[2], rsem.at[2], (row, (z + d) % 16)).start()

            zterms[z] = share[...]

        def send_back():
            plane_push(final, res.at[core, chip], ssem.at[3], rsem.at[3])
            res[core, chip] = final[...]

        def to_back():
            along.wait_recv()
            final[...] = total_of(zterms) * (1.0 / NSTATE)
            send_back()

        def to_half():
            back.wait_recv()
            half.start()

        def finish():
            for copy in [pair, spread, back, half] + ([] if along is None else [along]):
                copy.wait_send()

        return pair.start, to_plane, to_column, to_back, to_half, half.wait_recv, finish

    gather_start(0)
    old_step, old_finish = ring(old, oldall, og_s, og_r)
    old_step(0)
    oldall[z] = old[...]

    old_step(1)
    old_step(2)
    old_step(3)
    old_step(4)
    gather_product(0)

    a_start, a_plane, a_back, _, a_half, a_ready, a_finish = all_sum(
        apart, asib, ash, apl, None, None, afin, aout, a_s, a_r
    )

    def hook0(s):
        if 1 <= s <= 4:
            old_step(4 + s)
        if s == 5:
            every = oldall[...].reshape(512, 1024)
            for h in range(2):
                share = lax.dot_general(every[h * 256 : h * 256 + 256], every, NT, preferred_element_type=F32)
                apart[h] = share.reshape(16, 16, 512)
            a_start()
        if s == 6:
            a_plane()

    first_full = reduce_scatter(0, hook0)
    first[...] = first_full
    vsend[1] = first_full.astype(BF)
    gather_start(1)
    old_finish()
    winv[...] = jnp.zeros((768, 512), F32)
    upper[...] = jnp.zeros((768, 256), F32)
    inv2[...] = jnp.zeros((256, 256), F32)
    side = z % 2
    own_rows = lax.broadcasted_iota(jnp.int32, (128, 256), 0) // 64 == side

    def own_states(a):
        return jnp.where(own_rows, jnp.concatenate([a, a], 0), 0.0)

    gather_product(1)

    def assemble():
        a_ready()
        gram[...] = aout[...].reshape(512, 512)

    items = [assemble] + factor_items(gram, winv, turning, done, 4, 4)

    def work(count):
        for _ in range(min(count, len(items))):
            items.pop(0)()

    def hook1(s):
        if s == 1:
            a_back()
        if s == 5:
            a_half()
        if s == 7:
            work(2)

    second = reduce_scatter(1, hook1)
    vsend[2] = second.astype(BF)
    gather_start(2)

    work(8)
    gather_product(2)
    b_start, b_plane, b_column, b_back, b_half, b_ready, b_finish = all_sum(
        bpart, bsib, bs, br, bz, bsh, bfin, bout, b_s, b_r
    )

    def every_old():
        return oldall[...].reshape(512, 1024)

    def hook2(s):
        if s == 0:
            for t, piece in enumerate(split3(part[2].reshape(1024, 256) * -0.5)):
                bsplit[t] = piece
        if s <= 2:
            term = jnp.dot(every_old(), bsplit[s], preferred_element_type=F32)
            bacc[...] = term if s == 0 else bacc[...] + term
        if s == 2:
            cross = bacc[...]
            window = oldall[:, :, pl.ds(pl.multiple_of((z // 2) * 128, 128), 128)].reshape(512, 128)
            for t in split3(own_states(first[...] * 1.5)):
                cross = cross + jnp.dot(window, t, preferred_element_type=F32)
            bpart[...] = cross.reshape(2, 16, 16, 256)
            b_start()
        if s == 3:
            b_plane()
        if s == 6:
            b_column()
        if s in (4, 5, 7):
            work(1)

    third = reduce_scatter(2, hook2)
    panel = 1.5 * first[...] - 0.5 * third
    panel_o[...] = panel
    p_step, p_finish = ring(panel_o, pall, pg_s, pg_r)
    turned = panel.T
    cpart[...] = dot_nt(turned, turned).reshape(2, 16, 8, 256)
    c_start, c_plane, c_column, c_back, c_half, c_ready, c_finish = all_sum(
        cpart, csib, cs, cr, cz, csh, cfin, cout, c_s, c_r
    )
    c_start()
    p_step(0)
    pall[z] = panel
    c_plane()

    def to_lower():
        b_ready()
        lower[...] = dot_nt(bout[...].reshape(512, 256).T, winv[0:512, :])

    def to_square():
        square[...] = dot_nt(lower[...], lower[...])

    def to_onto():
        onto[...] = dot(lower[...], winv[0:512, :])

    def to_old_rows():
        res = jnp.zeros((48, 1024), F32)
        for t in split3(winv[pl.ds(pl.multiple_of(z * 48, 16), 48), :]):
            res = res + jnp.dot(t, every_old(), preferred_element_type=F32)
        basis_o[...] = res

    def to_rest():
        res = pall[...].reshape(1024, 256).T
        for t in split3(onto[...]):
            res = res - jnp.dot(t, every_old(), preferred_element_type=F32)
        tmat[...] = res

    items.extend([to_lower, to_square, to_onto, to_old_rows])
    b_back()
    p_step(1)
    work(3)
    c_column()
    p_step(2)
    work(2)
    b_half()
    p_step(3)
    work(2)
    p_step(4)
    work(2)
    c_back()
    p_step(5)
    work(2)
    p_step(6)
    work(1)
    c_half()
    p_step(7)
    work(100)
    p_step(8)
    to_rest()
    c_ready()
    gram2[...] = cout[...].reshape(256, 256) - square[...]
    for item in factor_items(gram2, inv2, turning, done, 2, 1):
        item()
    upper[512:768, :] = inv2[...]
    basis_o[...] += dot(upper[pl.ds(pl.multiple_of(z * 48, 16), 48), :], tmat[...])
    p_finish()
    a_finish()
    b_finish()
    c_finish()


def body(iterate_t, vectors, old_factor_t):
    vm = pl.BlockSpec(memory_space=pltpu.VMEM)
    dma = pltpu.SemaphoreType.DMA
    out = jax.ShapeDtypeStruct

    def f32(*shape):
        return pltpu.VMEM(shape, F32)

    return pl.pallas_call(
        comm_kernel,
        out_shape=(out((64, 256), F32), out((48, 1024), F32)),
        in_specs=[pl.BlockSpec(memory_space=pl.ANY), vm, vm],
        out_specs=(vm, vm),
        scratch_shapes=[
            pltpu.VMEM((32, 64, 1024), BF),
            pltpu.VMEM((1024, 2048), BF),
            pltpu.VMEM((3, 64, 256), BF),
            pltpu.VMEM((3, 32, 64, 256), BF),
            f32(3, 16, 64, 256), f32(3, 8, 64, 256), f32(3, 7, 64, 256), f32(64, 256),
            pltpu.VMEM((16, 32, 1024), BF), f32(16, 64, 256),
            f32(2, 16, 16, 512), f32(16, 16, 512), f32(16, 16, 512), f32(16, 16, 512), f32(16, 512), f32(2, 16, 16, 512),
            f32(512, 512), f32(128, 128), f32(128, 128), f32(768, 512),
            pltpu.VMEM((3, 1024, 256), BF), f32(512, 256),
            f32(2, 16, 16, 256), f32(16, 16, 256), f32(16, 16, 256), f32(16, 16, 256), f32(16, 16, 256),
            f32(16, 256), f32(16, 256), f32(2, 16, 16, 256),
            f32(2, 16, 8, 256), f32(16, 8, 256), f32(16, 8, 256), f32(16, 8, 256), f32(16, 8, 256),
            f32(8, 256), f32(8, 256), f32(2, 16, 8, 256),
            f32(256, 512), f32(256, 512), f32(256, 256), f32(256, 256), f32(256, 256), f32(768, 256),
            f32(256, 1024), dma((4,)),
            dma((3,)), dma((3,)), dma((3,)), dma((3,)),
            dma((3, 2, 8, 2)), dma((3, 2, 8, 2)),
            dma((2, 8)), dma((2, 8)),
            dma((2, 8)), dma((2, 8)),
            dma((5,)), dma((5,)), dma((5,)), dma((5,)), dma((5,)), dma((5,)),
        ],
        compiler_params=pltpu.CompilerParams(
            collective_id=0, has_side_effects=True, vmem_limit_bytes=56 << 20
        ),
        name="sign_step",
    )(iterate_t, vectors, old_factor_t)


def solution(mesh):
    return jax.shard_map(
        body,
        mesh=mesh,
        in_specs=(P(None, "col", None, "row"), P(("row", "col"), None), P("col", "row")),
        out_specs=(P(("row", "col"), None), P("col", "row")),
        check_vma=False,
    )
```

```python
import functools

import jax
import jax.numpy as jnp
from jax import lax
from jax.experimental import pallas as pl
from jax.experimental.pallas import tpu as pltpu
from jax.sharding import PartitionSpec as P

NSTATE = 32768
MESH = pl.DeviceIdType.MESH
HIGHEST = lax.Precision.HIGHEST
BF = jnp.bfloat16
F32 = jnp.float32
NT = (((1,), (1,)), ((), ()))


def split3(a):
    hi = a.astype(BF)
    rest = a - hi.astype(F32)
    mid = rest.astype(BF)
    low = (rest - mid.astype(F32)).astype(BF)
    return hi, mid, low


def eight(g, m, out):
    n = 128
    sub = lax.broadcasted_iota(jnp.int32, (8, n), 0)
    lane = lax.broadcasted_iota(jnp.int32, (8, n), 1)
    c = [jnp.broadcast_to(m[:8, 8 + k : 9 + k], (8, n)) for k in range(8)]
    turned = pltpu.roll(m, n - 8, 1)
    top = jnp.where(lane < 8, jnp.where(lane == sub, 1.0, 0.0), turned[:8])
    lines, steps, pivots = [], [], c[0]
    for s in range(8):
        if s:
            pivots = jnp.where(sub == s, c[s], pivots)
        inv = 1.0 / c[s][s : s + 1, :]
        line = top[s : s + 1, :] * inv
        col = jnp.where(sub > s, c[s], 0.0)
        top = top - col * line
        hs = [None] * 8
        for k in range(s + 1, 8):
            hs[k] = c[k][s : s + 1, :] * inv
            c[k] = c[k] - col * hs[k]
        lines.append(line)
        steps.append(hs)
    top = top * lax.rsqrt(pivots)
    top = jnp.where((lane < 8) | (lane >= n - 8 * g), top, 0.0)
    out[pl.ds(pl.multiple_of(g * 8, 8), 8), :] = pltpu.roll(top, 8 * g, 1)
    rest = []
    for r in range(1, 16):
        cr = [jnp.broadcast_to(m[8 * r : 8 * r + 8, 8 + k : 9 + k], (8, n)) for k in range(8)]
        acc = jnp.where(lane < 8, 0.0, turned[8 * r : 8 * r + 8])
        for s in range(8):
            for k in range(s + 1, 8):
                cr[k] = cr[k] - cr[s] * steps[s][k]
            acc = acc - cr[s] * lines[s]
        rest.append(acc)
    return jnp.concatenate(rest + [jnp.zeros((8, n), F32)], 0)


def dot(a, b):
    return jnp.dot(a, b, precision=HIGHEST, preferred_element_type=F32)


def dot_nt(a, b):
    return lax.dot_general(a, b, NT, precision=HIGHEST, preferred_element_type=F32)


def factor_items(gram, inv, turning, done, blocks, pieces):
    items = []
    size = blocks * 128
    for j in range(blocks):
        lo, hi = j * 128, (j + 1) * 128
        for p in range(pieces):

            def pivots(p=p, lo=lo, hi=hi):
                m = pltpu.roll(gram[lo:hi, lo:hi], 8, 1) if p == 0 else turning[...]
                step = 16 // pieces
                m = lax.fori_loop(p * step, (p + 1) * step, lambda g, m: eight(g, m, done), m)
                if p < pieces - 1:
                    turning[...] = m

            items.append(pivots)

        def rows(lo=lo, hi=hi):
            w = done[...]
            inv[lo:hi, lo:hi] = w
            if lo:
                inv[lo:hi, 0:lo] = dot(w, inv[lo:hi, 0:lo])
            if hi < size:
                gram[hi:size, lo:hi] = dot_nt(gram[hi:size, lo:hi], w)

        items.append(rows)
        if hi < size:

            def below(lo=lo, hi=hi):
                factor = gram[hi:size, lo:hi]
                for k in range(hi, size, 128):
                    gram[k:size, k : k + 128] -= dot_nt(factor[k - hi :], factor[k - hi : k - hi + 128])
                inv[hi:size, 0:hi] -= dot(factor, inv[lo:hi, 0:hi])

            items.append(below)
    return items


def comm_kernel(
    x, v, old, panel_o, basis_o,
    xs, xt, vsend, vg, part, bufr, bufl, first, oldall, pall,
    apart, asib, ash, apl, afin, aout, gram, turning, done, winv,
    bsplit, bacc, bpart, bsib, bs, br, bz, bsh, bfin, bout,
    cpart, csib, cs, cr, cz, csh, cfin, cout,
    lower, onto, square, gram2, inv2, upper, tmat, x_s,
    ag_s, ag_r, fw_s, fw_r, rs_s, rs_r, og_s, og_r, pg_s, pg_r,
    a_s, a_r, b_s, b_r, c_s, c_r,
):
    row = lax.axis_index("row")
    z = lax.axis_index("col")
    chip = row // 2
    core = row % 2
    sib = (chip * 2 + 1 - core, z)
    right = (row, (z + 1) % 16)
    left = (row, (z + 15) % 16)

    def plane(d):
        y = (chip // 4 + d // 4) % 4
        w = (chip % 4 + d % 4) % 4
        return y * 4 + w

    def remote(src, dst, ssem, rsem, target):
        return pltpu.make_async_remote_copy(
            src_ref=src, dst_ref=dst, send_sem=ssem, recv_sem=rsem, device_id=target, device_id_type=MESH
        )

    loads = [
        pltpu.make_async_copy(x.at[pl.ds(8 * q, 8), 0], xs.at[pl.ds(8 * q, 8)], x_s.at[q]) for q in range(4)
    ]
    for load in loads:
        load.start()
    barrier = pltpu.get_barrier_semaphore()

    @pl.loop(1, 16)
    def _(d):
        pl.semaphore_signal(barrier, inc=1, device_id=(plane(d) * 2 + core, z), device_id_type=MESH)
        pl.semaphore_signal(barrier, inc=1, device_id=(row, (z + d) % 16), device_id_type=MESH)

    pl.semaphore_signal(barrier, inc=1, device_id=sib, device_id_type=MESH)
    vsend[0] = v[...]

    for q in range(4):
        loads[q].wait()

        @pl.loop(0, 4)
        def _(u):
            a = 8 * q + (u // 2) * 4 + u % 2
            at = ((u % 2) * 8 + 2 * q + u // 2) * 128
            both = jnp.concatenate([xs[a], xs[a + 2]], 0)
            xt[:, pl.ds(pl.multiple_of(at, 128), 128)] = both.T

    pl.semaphore_wait(barrier, 31)

    def plane_push(src, dst, ssem, rsem):
        @pl.loop(1, 16)
        def _(d):
            remote(src, dst, ssem, rsem, (plane(d) * 2 + core, z)).start()

    def bulk(ref, ssem, rsem):
        return remote(ref.at[pl.ds(0, 15)], ref.at[pl.ds(0, 15)], ssem, rsem, sib)

    def gather_start(m):
        for d in (10, 9, 11, 6, 14, 2, 8, 5, 7, 13, 15, 1, 3, 4, 12):
            remote(
                vsend.at[m], vg.at[m, core * 16 + chip], ag_s.at[m], ag_r.at[m], (plane(d) * 2 + core, z)
            ).start()
        vg[m, core * 16 + chip] = vsend[m]

    def product(m, half, add):
        rhs = vg[m, pl.ds(half * 16, 16)].reshape(1024, 256)
        for rb in range(2):
            lhs = xt[pl.ds(rb * 512, 512), pl.ds(pl.multiple_of(half * 1024, 1024), 1024)]
            res = jnp.dot(lhs, rhs, preferred_element_type=F32).reshape(8, 64, 256)
            if add:
                part[m, pl.ds(rb * 8, 8)] += res
            else:
                part[m, pl.ds(rb * 8, 8)] = res

    def gather_product(m):
        wait = bulk(vg.at[m], ag_s.at[m], ag_r.at[m])
        wait.wait_recv()
        span = vg.at[m, pl.ds(core * 16, 16)]
        forward = remote(span, span, fw_s.at[m], fw_r.at[m], sib)
        forward.start()
        product(m, core, False)
        forward.wait_recv()
        product(m, 1 - core, True)
        wait.wait_send()
        forward.wait_send()

    def rs_copy(m, way, s, h):
        buf, to = (bufr, right) if way == 0 else (bufl, left)
        dest = (z + 8 - s) % 16 if way == 0 else (z + 9 + s) % 16
        rows = pl.ds(h * 32, 32)
        return remote(
            part.at[m, dest, rows], buf.at[m, s, rows], rs_s.at[m, way, s, h], rs_r.at[m, way, s, h], to
        ), dest

    def reduce_scatter(m, hook):
        for h in (0, 1):
            for way in (0, 1):
                rs_copy(m, way, 0, h)[0].start()
        hook(0)
        for s in range(1, 8):
            for h in (0, 1):
                for way in (0, 1):
                    if way == 1 and s == 7:
                        continue
                    rs_copy(m, way, s - 1, h)[0].wait_recv()
                    copy, dest = rs_copy(m, way, s, h)
                    rows = pl.ds(h * 32, 32)
                    part[m, dest, rows] += (bufr if way == 0 else bufl)[m, s - 1, rows]
                    copy.start()
            hook(s)
        for h in (0, 1):
            rs_copy(m, 1, 6, h)[0].wait_recv()
            rs_copy(m, 0, 7, h)[0].wait_recv()
        res = part[m, z] + bufr[m, 7] + bufl[m, 6]
        for h in (0, 1):
            for s in range(8):
                rs_copy(m, 0, s, h)[0].wait_send()
                if s < 7:
                    rs_copy(m, 1, s, h)[0].wait_send()
        return res

    def ring(own, blocks, ssem, rsem):
        def copy(way, s):
            idx = (z - s + 16) % 16 if way == 0 else (z + s) % 16
            return remote(
                own if s == 0 else blocks.at[idx], blocks.at[idx], ssem.at[way, s], rsem.at[way, s],
                right if way == 0 else left,
            )

        def step(s):
            for way in (0, 1):
                if s > 0 and not (way == 1 and s == 8):
                    copy(way, s - 1).wait_recv()
                if s < 8 and not (way == 1 and s == 7):
                    copy(way, s).start()

        def finish():
            for s in range(8):
                copy(0, s).wait_send()
                if s < 7:
                    copy(1, s).wait_send()

        return step, finish

    def total_of(parts):
        total = parts[0]
        for q in range(1, 16):
            total = total + parts[q]
        return total

    def all_sum(own, other, mine, terms, zterms, share, final, res, ssem, rsem):
        pair = remote(own.at[1 - core], other, ssem.at[0], rsem.at[0], sib)
        spread = bulk(terms, ssem.at[1], rsem.at[1])
        along = None if zterms is None else bulk(zterms, ssem.at[2], rsem.at[2])
        back = bulk(res.at[core], ssem.at[3], rsem.at[3])
        half = remote(res.at[core], res.at[core], ssem.at[4], rsem.at[4], sib)

        def to_plane():
            pair.wait_recv()
            mine[...] = own[core] + other[...]

            @pl.loop(1, 16)
            def _(d):
                q = plane(d)
                remote(mine.at[q], terms.at[chip], ssem.at[1], rsem.at[1], (q * 2 + core, z)).start()

            terms[chip] = mine[chip]

        def to_column():
            spread.wait_recv()
            if along is None:
                final[...] = total_of(terms) * (1.0 / NSTATE)
                send_back()
                return
            share[...] = total_of(terms)

            @pl.loop(1, 16)
            def _(d):
                remote(share, zterms.at[z], ssem.at[2], rsem.at[2], (row, (z + d) % 16)).start()

            zterms[z] = share[...]

        def send_back():
            plane_push(final, res.at[core, chip], ssem.at[3], rsem.at[3])
            res[core, chip] = final[...]

        def to_back():
            along.wait_recv()
            final[...] = total_of(zterms) * (1.0 / NSTATE)
            send_back()

        def to_half():
            back.wait_recv()
            half.start()

        def finish():
            for copy in [pair, spread, back, half] + ([] if along is None else [along]):
                copy.wait_send()

        return pair.start, to_plane, to_column, to_back, to_half, half.wait_recv, finish

    gather_start(0)
    old_step, old_finish = ring(old, oldall, og_s, og_r)
    old_step(0)
    oldall[z] = old[...]

    old_step(1)
    old_step(2)
    old_step(3)
    old_step(4)
    gather_product(0)

    a_start, a_plane, a_back, _, a_half, a_ready, a_finish = all_sum(
        apart, asib, ash, apl, None, None, afin, aout, a_s, a_r
    )

    def hook0(s):
        if 1 <= s <= 4:
            old_step(4 + s)
        if s == 5:
            every = oldall[...].reshape(512, 1024)
            for h in range(2):
                share = lax.dot_general(every[h * 256 : h * 256 + 256], every, NT, preferred_element_type=F32)
                apart[h] = share.reshape(16, 16, 512)
            a_start()
        if s == 6:
            a_plane()

    first_full = reduce_scatter(0, hook0)
    first[...] = first_full
    vsend[1] = first_full.astype(BF)
    gather_start(1)
    old_finish()
    winv[...] = jnp.zeros((768, 512), F32)
    upper[...] = jnp.zeros((768, 256), F32)
    inv2[...] = jnp.zeros((256, 256), F32)
    side = z % 2
    own_rows = lax.broadcasted_iota(jnp.int32, (128, 256), 0) // 64 == side

    def own_states(a):
        return jnp.where(own_rows, jnp.concatenate([a, a], 0), 0.0)

    gather_product(1)

    def assemble():
        a_ready()
        gram[...] = aout[...].reshape(512, 512)

    items = [assemble] + factor_items(gram, winv, turning, done, 4, 4)

    def work(count):
        for _ in range(min(count, len(items))):
            items.pop(0)()

    def hook1(s):
        if s == 1:
            a_back()
        if s == 5:
            a_half()
        if s == 7:
            work(2)

    second = reduce_scatter(1, hook1)
    vsend[2] = second.astype(BF)
    gather_start(2)

    work(8)
    gather_product(2)
    b_start, b_plane, b_column, b_back, b_half, b_ready, b_finish = all_sum(
        bpart, bsib, bs, br, bz, bsh, bfin, bout, b_s, b_r
    )

    def every_old():
        return oldall[...].reshape(512, 1024)

    def hook2(s):
        if s == 0:
            for t, piece in enumerate(split3(part[2].reshape(1024, 256) * -0.5)):
                bsplit[t] = piece
        if s <= 2:
            term = jnp.dot(every_old(), bsplit[s], preferred_element_type=F32)
            bacc[...] = term if s == 0 else bacc[...] + term
        if s == 2:
            cross = bacc[...]
            window = oldall[:, :, pl.ds(pl.multiple_of((z // 2) * 128, 128), 128)].reshape(512, 128)
            for t in split3(own_states(first[...] * 1.5)):
                cross = cross + jnp.dot(window, t, preferred_element_type=F32)
            bpart[...] = cross.reshape(2, 16, 16, 256)
            b_start()
        if s == 3:
            b_plane()
        if s in (4, 5, 6):
            work(1)

    third = reduce_scatter(2, hook2)
    panel = 1.5 * first[...] - 0.5 * third
    panel_o[...] = panel
    p_step, p_finish = ring(panel_o, pall, pg_s, pg_r)
    turned = panel.T
    cpart[...] = dot_nt(turned, turned).reshape(2, 16, 8, 256)
    c_start, c_plane, c_column, c_back, c_half, c_ready, c_finish = all_sum(
        cpart, csib, cs, cr, cz, csh, cfin, cout, c_s, c_r
    )
    c_start()
    p_step(0)
    pall[z] = panel
    c_plane()
    b_column()

    def to_lower():
        b_ready()
        lower[...] = dot_nt(bout[...].reshape(512, 256).T, winv[0:512, :])

    def to_square():
        square[...] = dot_nt(lower[...], lower[...])

    def to_onto():
        onto[...] = dot(lower[...], winv[0:512, :])

    def to_old_rows():
        res = jnp.zeros((48, 1024), F32)
        for t in split3(winv[pl.ds(pl.multiple_of(z * 48, 16), 48), :]):
            res = res + jnp.dot(t, every_old(), preferred_element_type=F32)
        basis_o[...] = res

    def to_rest():
        res = pall[...].reshape(1024, 256).T
        for t in split3(onto[...]):
            res = res - jnp.dot(t, every_old(), preferred_element_type=F32)
        tmat[...] = res

    items.extend([to_lower, to_square, to_onto, to_old_rows])
    p_step(1)
    work(3)
    c_column()
    p_step(2)
    work(2)
    b_back()
    p_step(3)
    work(2)
    p_step(4)
    work(2)
    c_back()
    b_half()
    p_step(5)
    work(2)
    p_step(6)
    work(1)
    c_half()
    p_step(7)
    work(100)
    c_ready()
    gram2[...] = cout[...].reshape(256, 256) - square[...]
    last = factor_items(gram2, inv2, turning, done, 2, 1)
    last[0]()
    p_step(8)
    to_rest()
    for item in last[1:]:
        item()
    upper[512:768, :] = inv2[...]
    basis_o[...] += dot(upper[pl.ds(pl.multiple_of(z * 48, 16), 48), :], tmat[...])
    p_finish()
    a_finish()
    b_finish()
    c_finish()


def body(iterate_t, vectors, old_factor_t):
    vm = pl.BlockSpec(memory_space=pltpu.VMEM)
    dma = pltpu.SemaphoreType.DMA
    out = jax.ShapeDtypeStruct

    def f32(*shape):
        return pltpu.VMEM(shape, F32)

    return pl.pallas_call(
        comm_kernel,
        out_shape=(out((64, 256), F32), out((48, 1024), F32)),
        in_specs=[pl.BlockSpec(memory_space=pl.ANY), vm, vm],
        out_specs=(vm, vm),
        scratch_shapes=[
            pltpu.VMEM((32, 64, 1024), BF),
            pltpu.VMEM((1024, 2048), BF),
            pltpu.VMEM((3, 64, 256), BF),
            pltpu.VMEM((3, 32, 64, 256), BF),
            f32(3, 16, 64, 256), f32(3, 8, 64, 256), f32(3, 7, 64, 256), f32(64, 256),
            pltpu.VMEM((16, 32, 1024), BF), f32(16, 64, 256),
            f32(2, 16, 16, 512), f32(16, 16, 512), f32(16, 16, 512), f32(16, 16, 512), f32(16, 512), f32(2, 16, 16, 512),
            f32(512, 512), f32(128, 128), f32(128, 128), f32(768, 512),
            pltpu.VMEM((3, 1024, 256), BF), f32(512, 256),
            f32(2, 16, 16, 256), f32(16, 16, 256), f32(16, 16, 256), f32(16, 16, 256), f32(16, 16, 256),
            f32(16, 256), f32(16, 256), f32(2, 16, 16, 256),
            f32(2, 16, 8, 256), f32(16, 8, 256), f32(16, 8, 256), f32(16, 8, 256), f32(16, 8, 256),
            f32(8, 256), f32(8, 256), f32(2, 16, 8, 256),
            f32(256, 512), f32(256, 512), f32(256, 256), f32(256, 256), f32(256, 256), f32(768, 256),
            f32(256, 1024), dma((4,)),
            dma((3,)), dma((3,)), dma((3,)), dma((3,)),
            dma((3, 2, 8, 2)), dma((3, 2, 8, 2)),
            dma((2, 8)), dma((2, 8)),
            dma((2, 8)), dma((2, 8)),
            dma((5,)), dma((5,)), dma((5,)), dma((5,)), dma((5,)), dma((5,)),
        ],
        compiler_params=pltpu.CompilerParams(
            collective_id=0, has_side_effects=True, vmem_limit_bytes=56 << 20
        ),
        name="sign_step",
    )(iterate_t, vectors, old_factor_t)


def solution(mesh):
    return jax.shard_map(
        body,
        mesh=mesh,
        in_specs=(P(None, "col", None, "row"), P(("row", "col"), None), P("col", "row")),
        out_specs=(P(("row", "col"), None), P("col", "row")),
        check_vma=False,
    )
```
